32 devices in a mesh: rad: 4 (over y, core), ang: 8 (over z, x).
Axes of the slice: x: 2, y: 2, z: 4, core: 2. Of those that a mesh axis runs over, the one named last changes fastest.
Arguments:
- source_coeffs: bfloat16 [512, 512, 2, 128], P('ang', 'rad'), may hold values from -6 to 6
- inverses: bfloat16 [512, 128, 128], P('rad')
- velocity: bfloat16 [2, 768, 128, 1536], P(None, 'ang', 'rad'), may hold values from -6 to 6
- order_slots: int32 [512], replicated, may hold values from 0 to 511, as said below
Outputs:
- advected: bfloat16 [512, 2, 128, 512], P('ang', None, 'rad')
The draws below stay inside these ranges and needn't reach their ends.
Inputs may be any that keep to these rules, and one draw needn't show every extreme that they name: `order_slots`: the slots form 512 // 64 consecutive blocks of 64; in each block the first 32 slots hold distinct orders below 256, and slot 32 + i of a block holds 511 minus the order in slot i of that block; every order appears exactly once.
All inputs are finite; a program needn't handle non-finite values.
Results may differ from the reference program's by a relative error of at most 0.012.
Values may be sent and summed in bfloat16 or wider, within the bound.
A program may use at most 320 MiB of HBM per device.

```python
import math
import jax
import jax.numpy as jnp
from jax import lax

LMAX = 512
NLAT = 768
NLON = 1536
NR = 128
K = 128
PAIRS = 32


def draw_inverses(key, part):
    first_key, second_key = jax.random.split(jax.random.fold_in(key, 11))
    degree_values = jnp.arange(LMAX, dtype=jnp.float32)
    mode_values = jnp.arange(K, dtype=jnp.float32)
    mixing = jax.random.normal(first_key, (LMAX, K, K), jnp.float32)
    jitter = jax.random.uniform(second_key, (LMAX, K), jnp.float32, 0.5, 2.0)
    core_matrix = jnp.eye(K, dtype=jnp.float32)[None] * jitter[:, :, None] + 0.6 * mixing / jnp.sqrt(K * 1.0)
    decay = 4.0 / ((degree_values + 1.0)[:, None, None] * ((1.0 + mode_values) ** 1.5)[None, :, None])
    return (core_matrix * decay).astype(jnp.bfloat16)


def draw_order_slots(key, part):
    lower_orders = jax.random.permutation(jax.random.fold_in(key, 23), LMAX // 2).astype(jnp.int32)
    grouped = lower_orders.reshape(LMAX // (2 * PAIRS), PAIRS)
    paired = jnp.concatenate([grouped, LMAX - 1 - grouped], 1)
    return paired.reshape(LMAX)


def level_of(rng, dims, cuts, low, high):
    loudness, own = 1.0, jax.random.fold_in(rng, 6)
    for dim, blocks in cuts:
        draws = jnp.exp(jax.random.uniform(jax.random.fold_in(own, dim), (blocks,), jnp.float32, low / len(cuts), high / len(cuts)))
        loudness = loudness * jnp.repeat(draws, dims[dim] // blocks).reshape([-1 if axis == dim else 1 for axis in range(len(dims))])
    return loudness


def bell_draw(rng, shape, scale, reach, cuts=(), held_as=jnp.bfloat16):
    drawn = jax.random.normal(rng, shape, jnp.float32) * scale
    if len(cuts) > 0:
        drawn = level_of(rng, shape, cuts, -0.22, 0.18) * drawn
    return jnp.clip(drawn, min=-reach, max=reach).astype(held_as)


def setup_inputs(seed: int = 0) -> dict:
    splits = jax.random.split(jax.random.key(seed), 5)
    return {
        "source_coeffs": bell_draw(splits[0], (LMAX, LMAX, 2, K), 1.0, 6.0, ((0, 8), (1, 4))),
        "inverses": draw_inverses(jax.random.fold_in(splits[4], 71), 0),
        "velocity": bell_draw(splits[2], (2, NLAT, NR, NLON), 1.0, 6.0, ((1, 8), (2, 4))),
        "order_slots": draw_order_slots(jax.random.fold_in(splits[4], 71), 0),
    }


inner_radius = 0.35
rescale_bound = 1e+20
rescale_log = 46.051701859880914
start_log = -1.2051210046670229

def round_keep(array_in):
    return lax.optimization_barrier(array_in.astype(jnp.bfloat16)).astype(jnp.float32)

def legendre_rows(orders, degree_count, lat_count):
    colatitude = (jnp.arange(lat_count, dtype=jnp.float32) + 0.5) * (math.pi / lat_count)
    cosines = jnp.cos(colatitude)[None, :]
    sines = jnp.sin(colatitude)[None, :]
    order_value = orders.astype(jnp.float32)[:, None]
    orders_col = orders.astype(jnp.int32)[:, None]
    log_start = start_log + 0.5 * (lax.lgamma(order_value + 1.5) - lax.lgamma(order_value + 1.0)) + order_value * jnp.log(sines)
    zero_field = jnp.zeros((orders.shape[0], lat_count), jnp.float32)

    def advance(state_carry, degree):
        prev_one, prev_two, log_scale = state_carry
        degree_value = degree.astype(jnp.float32)
        denominator = jnp.maximum(degree_value * degree_value - order_value * order_value, 1.0)
        recur_a = jnp.sqrt(jnp.maximum(4.0 * degree_value * degree_value - 1.0, 1.0) / denominator)
        lower_sq = (degree_value - 1.0) * (degree_value - 1.0)
        recur_b = jnp.sqrt(jnp.maximum(lower_sq - order_value * order_value, 0.0) / jnp.maximum(4.0 * lower_sq - 1.0, 1.0))
        grown_value = recur_a * (cosines * prev_one - recur_b * prev_two)
        before = degree < orders_col
        starting = degree == orders_col
        current = jnp.where(before, 0.0, jnp.where(starting, 1.0, grown_value))
        previous = jnp.where(before | starting, 0.0, prev_one)
        too_large = jnp.abs(current) > rescale_bound
        factor = jnp.where(too_large, 1.0 / rescale_bound, 1.0)
        log_scale = log_scale + jnp.where(too_large, rescale_log, 0.0)
        current = current * factor
        previous = previous * factor
        value_scaled = current * jnp.exp(log_scale)
        return ((current, previous, log_scale), value_scaled.astype(jnp.bfloat16))
    _, legendre = lax.scan(advance, (zero_field, zero_field, log_start + zero_field), jnp.arange(degree_count, dtype=jnp.int32))
    return legendre

def radial_tables(mode_count, radius_count):
    angles = (jnp.arange(radius_count, dtype=jnp.float32) + 0.5) * (math.pi / radius_count)
    mode_values = jnp.arange(mode_count, dtype=jnp.float32)[:, None]
    values = jnp.cos(mode_values * angles[None, :])
    slopes = mode_values * jnp.sin(mode_values * angles[None, :]) / jnp.sin(angles)[None, :] * (2.0 / (1.0 - inner_radius))
    return jnp.stack([values, slopes])

def fourier_tables(orders, lon_count):
    phase_index = orders.astype(jnp.int32)[:, None] * jnp.arange(lon_count, dtype=jnp.int32)[None, :] % lon_count
    phase_angle = phase_index.astype(jnp.float32) * (2.0 * math.pi / lon_count)
    weight = jnp.where(orders == 0, 1.0, 2.0).astype(jnp.float32)[:, None]
    cosine = jnp.cos(phase_angle)
    sine = jnp.sin(phase_angle)
    synth_table = jnp.stack([weight * cosine, -weight * sine], 1).astype(jnp.bfloat16)
    analyse_table = (jnp.stack([cosine, -sine], 1) * (2.0 * math.pi / lon_count)).astype(jnp.bfloat16)
    return (synth_table, analyse_table)

def reference(source_coeffs, inverses, velocity, order_slots):
    slot_count, degree_count, _, mode_count = source_coeffs.shape
    lat_count = velocity.shape[1]
    radius_count = velocity.shape[2]
    lon_count = velocity.shape[3]
    degrees = jnp.arange(degree_count, dtype=jnp.int32)
    degree_mask = (degrees[None, :] >= order_slots[:, None]).astype(jnp.float32)
    solved = jnp.einsum('lkj,slcj->slck', inverses.astype(jnp.float32), source_coeffs.astype(jnp.float32), precision=lax.Precision.HIGHEST) * degree_mask[:, :, None, None]
    tables = radial_tables(mode_count, radius_count)
    synth_table, analyse_table = fourier_tables(order_slots, lon_count)
    colatitude = (jnp.arange(lat_count, dtype=jnp.float32) + 0.5) * (math.pi / lat_count)
    sines = jnp.sin(colatitude)
    quad_weight = math.pi / lat_count * sines
    angles = (jnp.arange(radius_count, dtype=jnp.float32) + 0.5) * (math.pi / radius_count)
    radius_values = inner_radius + (1.0 - inner_radius) * (jnp.cos(angles) + 1.0) * 0.5
    order_value = order_slots.astype(jnp.float32)
    block_size = min(32, slot_count)
    slot_blocks = slot_count // block_size
    radius_block = min(16, radius_count)
    radius_blocks = radius_count // radius_block

    def radius_piece(start):
        table_piece = lax.dynamic_slice_in_dim(tables, start, radius_block, 2)
        radius_local = lax.dynamic_slice_in_dim(radius_values, start, radius_block, 0)
        velocity_piece = lax.dynamic_slice_in_dim(velocity, start, radius_block, 2).astype(jnp.float32)

        def synth_block(slot_block):
            first_slot = slot_block * block_size
            orders = lax.dynamic_slice_in_dim(order_slots, first_slot, block_size, 0)
            legendre = legendre_rows(orders, degree_count, lat_count).astype(jnp.float32)
            solved_piece = lax.dynamic_slice_in_dim(solved, first_slot, block_size, 0)
            radial = round_keep(jnp.einsum('slck,fki->sfcli', solved_piece, table_piece, precision=lax.Precision.HIGHEST))
            lat_spec = round_keep(jnp.einsum('sfcli,lsj->sfcij', radial, legendre))
            order_piece = lax.dynamic_slice_in_dim(order_value, first_slot, block_size, 0)[:, None, None]
            azim = jnp.stack([-order_piece * lat_spec[:, 0, 1], order_piece * lat_spec[:, 0, 0]], 1)
            azim = round_keep(azim)
            return jnp.concatenate([lat_spec, azim[:, None]], 1)
        fields = lax.map(synth_block, jnp.arange(slot_blocks)).reshape(slot_count, 3, 2, radius_block, lat_count)
        physical = jnp.einsum('sfcij,scn->fjin', fields, synth_table.astype(jnp.float32))
        radius_col = radius_local[None, :, None]
        flux_term = velocity_piece[0] * (physical[1] + 3.0 * physical[0] / radius_col) + velocity_piece[1] * physical[2] / (radius_col * sines[:, None, None])
        flux_term = round_keep(flux_term)
        fourier = jnp.einsum('jin,scn->scij', flux_term, analyse_table.astype(jnp.float32))
        fourier = round_keep(fourier * quad_weight[None, None, None, :])

        def analyse_block(slot_block):
            first_slot = slot_block * block_size
            orders = lax.dynamic_slice_in_dim(order_slots, first_slot, block_size, 0)
            legendre = legendre_rows(orders, degree_count, lat_count).astype(jnp.float32)
            fourier_piece = lax.dynamic_slice_in_dim(fourier, first_slot, block_size, 0)
            return jnp.einsum('scij,lsj->scil', fourier_piece, legendre).astype(jnp.bfloat16)
        return lax.map(analyse_block, jnp.arange(slot_blocks)).reshape(slot_count, 2, radius_block, degree_count)
    pieces = lax.map(radius_piece, jnp.arange(radius_blocks, dtype=jnp.int32) * radius_block)
    return pieces.transpose(1, 2, 0, 3, 4).reshape(slot_count, 2, radius_count, degree_count)
```

```python
import functools
import math

import jax
import jax.numpy as jnp
from jax import lax
from jax.experimental import pallas as pl
from jax.experimental.pallas import tpu as pltpu
from jax.sharding import PartitionSpec as P

inner_radius = 0.35
rescale_bound = 1e8
rescale_factor = 1e-20
rescale_log = 46.051701859880914
start_log = -1.2051210046670229


def legendre_kernel(chunk, recur_a_ref, recur_ab_ref, orders_ref, log_start_ref, cosines_ref, out_ref, cur_ref, prev_ref, log_ref):
    step_count, slots, lat_count = out_ref.shape
    lanes = recur_a_ref.shape[2]
    tiles = lat_count // lanes
    degree_block = pl.program_id(1)

    @pl.when(degree_block == 0)
    def _():
        cur_ref[...] = jnp.zeros_like(cur_ref)
        prev_ref[...] = jnp.zeros_like(prev_ref)
        log_ref[...] = log_start_ref[...]

    orders = orders_ref[...]

    def run_chunk(index, carry):
        for tile in range(tiles):
            columns = slice(tile * lanes, (tile + 1) * lanes)
            cur, prev, log_scale = cur_ref[:, columns], prev_ref[:, columns], log_ref[:, columns]
            too_large = jnp.abs(cur) > rescale_bound
            factor = jnp.where(too_large, rescale_factor, 1.0)
            log_scale = log_scale + jnp.where(too_large, rescale_log, 0.0)
            cur, prev = cur * factor, prev * factor
            scale = jnp.exp(log_scale)
            cosines = cosines_ref[:, columns]
            for inner in range(chunk):
                step = index * chunk + inner
                starting = orders == degree_block * step_count + step
                grown = recur_a_ref[step] * (cosines * cur) - recur_ab_ref[step] * prev
                cur, prev = jnp.where(starting, 1.0, grown), cur
                out_ref[step, :, columns] = (cur * scale).astype(jnp.bfloat16)
            cur_ref[:, columns] = cur
            prev_ref[:, columns] = prev
            log_ref[:, columns] = log_scale
        return carry

    lax.fori_loop(0, step_count // chunk, run_chunk, 0)


def legendre_rows(orders, degree_count, lat_count):
    slot_count = orders.shape[0]
    lanes, chunk, slot_block, degree_block = 128, 8, 16, 64
    colatitude = (jnp.arange(lat_count, dtype=jnp.float32) + 0.5) * (math.pi / lat_count)
    cosines = jnp.broadcast_to(jnp.cos(colatitude)[None, :], (slot_block, lat_count))
    sines = jnp.sin(colatitude)[None, :]
    order_value = orders.astype(jnp.float32)[:, None]
    log_start = (
        start_log
        + 0.5 * (lax.lgamma(order_value + 1.5) - lax.lgamma(order_value + 1.0))
        + order_value * jnp.log(sines)
    )
    degree_value = jnp.arange(degree_count, dtype=jnp.float32)[:, None]
    order_row = order_value[:, 0][None, :]
    denominator = jnp.maximum(degree_value * degree_value - order_row * order_row, 1.0)
    recur_a = jnp.sqrt(jnp.maximum(4.0 * degree_value * degree_value - 1.0, 1.0) / denominator)
    lower_sq = (degree_value - 1.0) * (degree_value - 1.0)
    recur_b = jnp.sqrt(
        jnp.maximum(lower_sq - order_row * order_row, 0.0) / jnp.maximum(4.0 * lower_sq - 1.0, 1.0)
    )
    table_shape = (degree_count, slot_count, lanes)
    recur_ab = jnp.broadcast_to((recur_a * recur_b)[:, :, None], table_shape)
    recur_a = jnp.broadcast_to(recur_a[:, :, None], table_shape)
    order_tile = jnp.broadcast_to(orders[:, None], (slot_count, lanes))
    table_spec = pl.BlockSpec((degree_block, slot_block, lanes), lambda s, l: (l, s, 0))
    state = pltpu.VMEM((slot_block, lat_count), jnp.float32)
    return pl.pallas_call(
        functools.partial(legendre_kernel, chunk),
        grid=(slot_count // slot_block, degree_count // degree_block),
        in_specs=[
            table_spec,
            table_spec,
            pl.BlockSpec((slot_block, lanes), lambda s, l: (s, 0)),
            pl.BlockSpec((slot_block, lat_count), lambda s, l: (s, 0)),
            pl.BlockSpec((slot_block, lat_count), lambda s, l: (0, 0)),
        ],
        out_specs=pl.BlockSpec((degree_block, slot_block, lat_count), lambda s, l: (l, s, 0)),
        out_shape=jax.ShapeDtypeStruct((degree_count, slot_count, lat_count), jnp.bfloat16),
        scratch_shapes=[state, state, state],
        compiler_params=pltpu.CompilerParams(vmem_limit_bytes=32 * 1024 * 1024),
        cost_estimate=pl.CostEstimate(
            flops=8 * degree_count * slot_count * lat_count,
            bytes_accessed=2 * degree_count * slot_count * (lat_count + 4 * lanes),
            transcendentals=degree_count * slot_count * lat_count // chunk,
        ),
        name="legendre",
    )(recur_a, recur_ab, order_tile, log_start, cosines)


def radial_tables(mode_count, radius_count):
    angles = (jnp.arange(radius_count, dtype=jnp.float32) + 0.5) * (math.pi / radius_count)
    mode_values = jnp.arange(mode_count, dtype=jnp.float32)[:, None]
    values = jnp.cos(mode_values * angles[None, :])
    slopes = (
        mode_values
        * jnp.sin(mode_values * angles[None, :])
        / jnp.sin(angles)[None, :]
        * (2.0 / (1.0 - inner_radius))
    )
    radii = inner_radius + (1.0 - inner_radius) * (jnp.cos(angles) + 1.0) * 0.5
    return jnp.stack([values, slopes + 3.0 * values / radii[None, :]])


def fourier_tables(orders, lon_count):
    phase_index = orders[:, None] * jnp.arange(lon_count, dtype=jnp.int32)[None, :] % lon_count
    phase_angle = phase_index.astype(jnp.float32) * (2.0 * math.pi / lon_count)
    weight = jnp.where(orders == 0, 1.0, 2.0).astype(jnp.float32)[:, None]
    cosine = jnp.cos(phase_angle)
    sine = jnp.sin(phase_angle)
    order_value = orders.astype(jnp.float32)[:, None]
    synth_table = jnp.stack([weight * cosine, -weight * sine], 1).astype(jnp.bfloat16)
    turn_table = jnp.stack(
        [-order_value * weight * sine, -order_value * weight * cosine], 1
    ).astype(jnp.bfloat16)
    analyse_table = (jnp.stack([cosine, -sine], 1) * (2.0 * math.pi / lon_count)).astype(
        jnp.bfloat16
    )
    return (synth_table, turn_table, analyse_table)


def local(source_coeffs, inverses, velocity, order_slots):
    slots_local, degrees_local, _, mode_count = source_coeffs.shape
    lat_local = velocity.shape[1]
    radii_local = velocity.shape[2]
    lon_count = velocity.shape[3]
    rad_count = lax.axis_size("rad")
    ang_count = lax.axis_size("ang")
    degree_count = degrees_local * rad_count
    lat_count = lat_local * ang_count
    radius_count = radii_local * rad_count
    rad_index = lax.axis_index("rad")
    ang_index = lax.axis_index("ang")
    my_orders = lax.dynamic_slice_in_dim(order_slots, ang_index * slots_local, slots_local, 0)
    degrees = rad_index * degrees_local + jnp.arange(degrees_local, dtype=jnp.int32)
    degree_mask = (degrees[None, :] >= my_orders[:, None]).astype(jnp.float32)
    solved = (
        jnp.einsum("lkj,slcj->slck", inverses, source_coeffs, preferred_element_type=jnp.float32)
        * degree_mask[:, :, None, None]
    )
    tables = radial_tables(mode_count, radius_count)
    radial = jnp.einsum("slck,fki->sfcli", solved, tables, precision=lax.Precision.HIGHEST).astype(
        jnp.bfloat16
    )
    radial = lax.all_to_all(radial, "rad", split_axis=4, concat_axis=3, tiled=True)
    legendre = legendre_rows(my_orders, degree_count, lat_count)
    lat_spec = jnp.einsum(
        "sfcli,lsj->sjfci", radial, legendre, preferred_element_type=jnp.float32
    ).astype(jnp.bfloat16)
    lat_spec = lat_spec.reshape(slots_local, lat_count, 4 * radii_local)
    received = lax.all_to_all(lat_spec, "ang", split_axis=1, concat_axis=0, tiled=True)
    slot_count = slots_local * ang_count
    fields = received.reshape(slot_count, lat_local, 2, 2, radii_local)
    synth_table, turn_table, analyse_table = fourier_tables(order_slots, lon_count)
    turn = jnp.einsum(
        "sjci,scn->jin", fields[:, :, 0], turn_table, preferred_element_type=jnp.float32
    )
    growth = jnp.einsum(
        "sjci,scn->jin", fields[:, :, 1], synth_table, preferred_element_type=jnp.float32
    )
    lat_rows = ang_index * lat_local + jnp.arange(lat_local, dtype=jnp.int32)
    colatitude = (lat_rows.astype(jnp.float32) + 0.5) * (math.pi / lat_count)
    sines = jnp.sin(colatitude)
    quad_weight = math.pi / lat_count * sines
    radius_rows = rad_index * radii_local + jnp.arange(radii_local, dtype=jnp.int32)
    angles = (radius_rows.astype(jnp.float32) + 0.5) * (math.pi / radius_count)
    radius_col = (inner_radius + (1.0 - inner_radius) * (jnp.cos(angles) + 1.0) * 0.5)[
        None, :, None
    ]
    flux_term = velocity[0].astype(jnp.float32) * growth + velocity[1].astype(jnp.float32) * (
        turn / (radius_col * sines[:, None, None])
    )
    flux_term = flux_term.astype(jnp.bfloat16).reshape(lat_local * radii_local, lon_count)
    analyse_table = analyse_table.reshape(slot_count * 2, lon_count)
    fourier = jnp.einsum("qn,pn->pq", flux_term, analyse_table, preferred_element_type=jnp.float32)
    weight_row = jnp.repeat(quad_weight, radii_local)
    fourier = (fourier * weight_row[None, :]).astype(jnp.bfloat16)
    fourier = lax.all_to_all(fourier, "ang", split_axis=0, concat_axis=1, tiled=True)
    fourier = fourier.reshape(slots_local, 2, lat_count, radii_local)
    advected = jnp.einsum(
        "scji,lsj->scil", fourier, legendre, preferred_element_type=jnp.float32
    ).astype(jnp.bfloat16)
    return advected


def solution(mesh):
    in_specs = (P("ang", "rad", None, None), P("rad", None, None), P(None, "ang", "rad", None), P())
    out_specs = P("ang", None, "rad", None)
    return jax.shard_map(local, mesh=mesh, in_specs=in_specs, out_specs=out_specs, check_vma=False)
```

```python
import functools
import math

import jax
import jax.numpy as jnp
from jax import lax
from jax.experimental import pallas as pl
from jax.experimental.pallas import tpu as pltpu
from jax.sharding import PartitionSpec as P

inner_radius = 0.35
rescale_bound = 1e8
rescale_factor = 1e-20
rescale_log = 46.051701859880914
start_log = -1.2051210046670229


def legendre_kernel(chunk, recur_a_ref, recur_ab_ref, orders_ref, log_start_ref, cosines_ref, out_ref, cur_ref, prev_ref, log_ref):
    step_count, slots, lat_count = out_ref.shape
    lanes = recur_a_ref.shape[2]
    tiles = lat_count // lanes
    degree_block = pl.program_id(1)

    @pl.when(degree_block == 0)
    def _():
        cur_ref[...] = jnp.zeros_like(cur_ref)
        prev_ref[...] = jnp.zeros_like(prev_ref)
        log_ref[...] = log_start_ref[...]

    orders = orders_ref[...]

    def run_chunk(index, carry):
        for tile in range(tiles):
            columns = slice(tile * lanes, (tile + 1) * lanes)
            cur, prev, log_scale = cur_ref[:, columns], prev_ref[:, columns], log_ref[:, columns]
            too_large = jnp.abs(cur) > rescale_bound
            factor = jnp.where(too_large, rescale_factor, 1.0)
            log_scale = log_scale + jnp.where(too_large, rescale_log, 0.0)
            cur, prev = cur * factor, prev * factor
            scale = jnp.exp(log_scale)
            cosines = cosines_ref[:, columns]
            for inner in range(chunk):
                step = index * chunk + inner
                starting = orders == degree_block * step_count + step
                grown = recur_a_ref[step] * (cosines * cur) - recur_ab_ref[step] * prev
                cur, prev = jnp.where(starting, 1.0, grown), cur
                out_ref[step, :, columns] = (cur * scale).astype(jnp.bfloat16)
            cur_ref[:, columns] = cur
            prev_ref[:, columns] = prev
            log_ref[:, columns] = log_scale
        return carry

    lax.fori_loop(0, step_count // chunk, run_chunk, 0)


def legendre_rows(orders, degree_count, lat_count):
    slot_count = orders.shape[0]
    lanes, chunk, slot_block, degree_block = 128, 8, 16, 64
    colatitude = (jnp.arange(lat_count, dtype=jnp.float32) + 0.5) * (math.pi / lat_count)
    cosines = jnp.broadcast_to(jnp.cos(colatitude)[None, :], (slot_block, lat_count))
    sines = jnp.sin(colatitude)[None, :]
    order_value = orders.astype(jnp.float32)[:, None]
    log_start = (
        start_log
        + 0.5 * (lax.lgamma(order_value + 1.5) - lax.lgamma(order_value + 1.0))
        + order_value * jnp.log(sines)
    )
    degree_value = jnp.arange(degree_count, dtype=jnp.float32)[:, None]
    order_row = order_value[:, 0][None, :]
    denominator = jnp.maximum(degree_value * degree_value - order_row * order_row, 1.0)
    recur_a = jnp.sqrt(jnp.maximum(4.0 * degree_value * degree_value - 1.0, 1.0) / denominator)
    lower_sq = (degree_value - 1.0) * (degree_value - 1.0)
    recur_b = jnp.sqrt(
        jnp.maximum(lower_sq - order_row * order_row, 0.0) / jnp.maximum(4.0 * lower_sq - 1.0, 1.0)
    )
    table_shape = (degree_count, slot_count, lanes)
    recur_ab = jnp.broadcast_to((recur_a * recur_b)[:, :, None], table_shape)
    recur_a = jnp.broadcast_to(recur_a[:, :, None], table_shape)
    order_tile = jnp.broadcast_to(orders[:, None], (slot_count, lanes))
    table_spec = pl.BlockSpec((degree_block, slot_block, lanes), lambda s, l: (l, s, 0))
    state = pltpu.VMEM((slot_block, lat_count), jnp.float32)
    return pl.pallas_call(
        functools.partial(legendre_kernel, chunk),
        grid=(slot_count // slot_block, degree_count // degree_block),
        in_specs=[
            table_spec,
            table_spec,
            pl.BlockSpec((slot_block, lanes), lambda s, l: (s, 0)),
            pl.BlockSpec((slot_block, lat_count), lambda s, l: (s, 0)),
            pl.BlockSpec((slot_block, lat_count), lambda s, l: (0, 0)),
        ],
        out_specs=pl.BlockSpec((degree_block, slot_block, lat_count), lambda s, l: (l, s, 0)),
        out_shape=jax.ShapeDtypeStruct((degree_count, slot_count, lat_count), jnp.bfloat16),
        scratch_shapes=[state, state, state],
        compiler_params=pltpu.CompilerParams(vmem_limit_bytes=32 * 1024 * 1024),
        cost_estimate=pl.CostEstimate(
            flops=8 * degree_count * slot_count * lat_count,
            bytes_accessed=2 * degree_count * slot_count * (lat_count + 4 * lanes),
            transcendentals=degree_count * slot_count * lat_count // chunk,
        ),
        name="legendre",
    )(recur_a, recur_ab, order_tile, log_start, cosines)


def radial_tables(mode_count, radius_count):
    angles = (jnp.arange(radius_count, dtype=jnp.float32) + 0.5) * (math.pi / radius_count)
    mode_values = jnp.arange(mode_count, dtype=jnp.float32)[:, None]
    values = jnp.cos(mode_values * angles[None, :])
    slopes = (
        mode_values
        * jnp.sin(mode_values * angles[None, :])
        / jnp.sin(angles)[None, :]
        * (2.0 / (1.0 - inner_radius))
    )
    radii = inner_radius + (1.0 - inner_radius) * (jnp.cos(angles) + 1.0) * 0.5
    return jnp.stack([values, slopes + 3.0 * values / radii[None, :]])


def fourier_tables(orders, lon_count):
    phase_index = orders[:, None] * jnp.arange(lon_count, dtype=jnp.int32)[None, :] % lon_count
    phase_angle = phase_index.astype(jnp.float32) * (2.0 * math.pi / lon_count)
    weight = jnp.where(orders == 0, 1.0, 2.0).astype(jnp.float32)[:, None]
    cosine = jnp.cos(phase_angle)
    sine = jnp.sin(phase_angle)
    order_value = orders.astype(jnp.float32)[:, None]
    synth_table = jnp.stack([weight * cosine, -weight * sine], 1).astype(jnp.bfloat16)
    turn_table = jnp.stack(
        [-order_value * weight * sine, -order_value * weight * cosine], 1
    ).astype(jnp.bfloat16)
    analyse_table = (jnp.stack([cosine, -sine], 1) * (2.0 * math.pi / lon_count)).astype(
        jnp.bfloat16
    )
    return (synth_table, turn_table, analyse_table)


def local(source_coeffs, inverses, velocity, order_slots):
    slots_local, degrees_local, _, mode_count = source_coeffs.shape
    lat_local = velocity.shape[1]
    radii_local = velocity.shape[2]
    lon_count = velocity.shape[3]
    rad_count = lax.axis_size("rad")
    ang_count = lax.axis_size("ang")
    degree_count = degrees_local * rad_count
    lat_count = lat_local * ang_count
    radius_count = radii_local * rad_count
    rad_index = lax.axis_index("rad")
    ang_index = lax.axis_index("ang")
    my_orders = lax.dynamic_slice_in_dim(order_slots, ang_index * slots_local, slots_local, 0)
    degrees = rad_index * degrees_local + jnp.arange(degrees_local, dtype=jnp.int32)
    degree_mask = (degrees[None, :] >= my_orders[:, None]).astype(jnp.float32)
    solved = (
        jnp.einsum("lkj,slcj->slck", inverses, source_coeffs, preferred_element_type=jnp.float32)
        * degree_mask[:, :, None, None]
    )
    tables = radial_tables(mode_count, radius_count)
    radial = jnp.einsum("slck,fki->sfcli", solved, tables, precision=lax.Precision.HIGHEST).astype(
        jnp.bfloat16
    )
    radial = lax.all_to_all(radial, "rad", split_axis=4, concat_axis=3, tiled=True)
    parts = 2
    part_slots = slots_local // parts
    slot_count = part_slots * ang_count
    grouped_orders = order_slots.reshape(ang_count, parts, part_slots)
    legendre, received, tables_of = [], [], []
    for part in range(parts):
        own = slice(part * part_slots, (part + 1) * part_slots)
        legendre.append(legendre_rows(my_orders[own], degree_count, lat_count))
        lat_spec = jnp.einsum(
            "sfcli,lsj->sjfci", radial[own], legendre[part], preferred_element_type=jnp.float32
        ).astype(jnp.bfloat16)
        lat_spec = lat_spec.reshape(part_slots, lat_count, 4 * radii_local)
        received.append(lax.all_to_all(lat_spec, "ang", split_axis=1, concat_axis=0, tiled=True))
        tables_of.append(fourier_tables(grouped_orders[:, part].reshape(-1), lon_count))
    turn, growth = 0.0, 0.0
    for part in range(parts):
        fields = received[part].reshape(slot_count, lat_local, 2, 2, radii_local)
        synth_table, turn_table, _ = tables_of[part]
        turn += jnp.einsum(
            "sjci,scn->jin", fields[:, :, 0], turn_table, preferred_element_type=jnp.float32
        )
        growth += jnp.einsum(
            "sjci,scn->jin", fields[:, :, 1], synth_table, preferred_element_type=jnp.float32
        )
    lat_rows = ang_index * lat_local + jnp.arange(lat_local, dtype=jnp.int32)
    colatitude = (lat_rows.astype(jnp.float32) + 0.5) * (math.pi / lat_count)
    sines = jnp.sin(colatitude)
    quad_weight = math.pi / lat_count * sines
    radius_rows = rad_index * radii_local + jnp.arange(radii_local, dtype=jnp.int32)
    angles = (radius_rows.astype(jnp.float32) + 0.5) * (math.pi / radius_count)
    radius_col = (inner_radius + (1.0 - inner_radius) * (jnp.cos(angles) + 1.0) * 0.5)[
        None, :, None
    ]
    flux_term = velocity[0].astype(jnp.float32) * growth + velocity[1].astype(jnp.float32) * (
        turn / (radius_col * sines[:, None, None])
    )
    flux_term = flux_term.astype(jnp.bfloat16).reshape(lat_local * radii_local, lon_count)
    weight_row = jnp.repeat(quad_weight, radii_local)
    exchanged = []
    for part in range(parts):
        analyse_table = tables_of[part][2].reshape(slot_count * 2, lon_count)
        fourier = jnp.einsum(
            "qn,pn->pq", flux_term, analyse_table, preferred_element_type=jnp.float32
        )
        fourier = (fourier * weight_row[None, :]).astype(jnp.bfloat16)
        exchanged.append(lax.all_to_all(fourier, "ang", split_axis=0, concat_axis=1, tiled=True))
    advected = []
    for part in range(parts):
        fourier = exchanged[part].reshape(part_slots, 2, lat_count, radii_local)
        fourier = lax.optimization_barrier(fourier.transpose(0, 1, 3, 2))
        advected.append(
            jnp.einsum(
                "scij,lsj->scil", fourier, legendre[part], preferred_element_type=jnp.float32
            ).astype(jnp.bfloat16)
        )
    return jnp.concatenate(advected, 0)


def solution(mesh):
    in_specs = (P("ang", "rad", None, None), P("rad", None, None), P(None, "ang", "rad", None), P())
    out_specs = P("ang", None, "rad", None)
    return jax.shard_map(local, mesh=mesh, in_specs=in_specs, out_specs=out_specs, check_vma=False)
```
